1024 devices in a mesh: tok: 128 (over x, z), head: 4 (over y), srv: 2 (over core).
Axes of the slice: x: 4, y: 4, z: 32, core: 2. Of those that a mesh axis runs over, the one named last changes fastest.
Arguments:
- queries: bfloat16 [32768, 4096], P('tok', ('head', 'srv')), may hold values from -12 to 12
- key_heads: bfloat16 [32768, 1024], P('tok', ('head', 'srv')), may hold values from -12 to 12
- value_heads: bfloat16 [32768, 1024], P('tok', ('head', 'srv')), may hold values from -6 to 6
- doc_ids: int32 [32768], P('tok'), may hold values from 0 to 15, never falling along the last dimension, each value on 1 to 3840 neighbouring positions
- out_weight: bfloat16 [4096, 4096], P(('head', 'srv')), may hold values from -0.125 to 0.125
Outputs:
- mixed: bfloat16 [32768, 4096], P('tok', ('head', 'srv'))
The draws below stay inside these ranges and needn't reach their ends.
Inputs may be any that keep to these rules, and one draw needn't show every extreme that they name: `doc_ids`: document ids never fall along the window; every document holds 1 to 3840 tokens, and one holds exactly 3840.
All inputs are finite; a program needn't handle non-finite values.
Results may differ from the reference program's by a relative error of at most 0.019.
Values may be sent and summed in bfloat16 or wider, within the bound.
No kernel may reach another device: no remote copies, remote signals or barrier semaphores. Data moves between devices by JAX's collectives and lax.ppermute only.
A program may use at most 32 MiB of HBM per device.

```python
import math
import jax
import jax.numpy as jnp
import numpy as np
from jax import lax

D = 4096
HEADS = 32
KV_HEADS = 8
HEAD_DIM = 128
TOK_DEV = 256
DOCS = 16
DOC_MAX = 3840
TOKENS = 32768


def paired_heads(key):
    folded = jax.random.fold_in(key, 11)
    sub_query, sub_key = jax.random.split(folded, 2)
    group_size = HEADS // KV_HEADS
    query_shape = (TOKENS, KV_HEADS, group_size, HEAD_DIM)
    key_shape = (TOKENS, KV_HEADS, HEAD_DIM)
    query_vals = jnp.clip(1.5 * jax.random.normal(sub_query, query_shape, jnp.float32), -9.0, 9.0)
    key_vals = jnp.clip(1.5 * jax.random.normal(sub_key, key_shape, jnp.float32), -9.0, 9.0)
    return (query_vals.reshape(TOKENS, HEADS * HEAD_DIM), key_vals.reshape(TOKENS, KV_HEADS * HEAD_DIM))


def draw_queries(key, part):
    return paired_heads(key)[0].astype(jnp.bfloat16)


def draw_key_heads(key, part):
    return paired_heads(key)[1].astype(jnp.bfloat16)


def strengthened(array, own_key, source, target, blocks, factor):
    def block_of(dim):
        return (jnp.arange(array.shape[dim]) // (array.shape[dim] // blocks)).reshape((-1,) + (1,) * (array.ndim - 1 - dim))

    one_side = jax.random.permutation(own_key, blocks)[block_of(target)]
    second = (block_of(target) + blocks // 2) % blocks
    return jnp.where((block_of(source) == one_side) | (block_of(source) == second), factor * array, array)


def block_levels(own_key, dims, shards, least, high):
    loudness = 1.0
    for axis_at, parts in shards:
        draws = jax.random.uniform(jax.random.fold_in(jax.random.fold_in(own_key, 6), axis_at), (parts,), jnp.float32, least / len(shards), high / len(shards))
        loudness = loudness * jnp.repeat(jnp.exp(draws), dims[axis_at] // parts).reshape((-1,) + (1,) * (len(dims) - 1 - axis_at))
    return loudness


def length_profile(amount, total, bound, lean):
    weights = [(1 << 20) // math.isqrt(standing ** lean) + 1 for standing in range(2, amount + 1)]
    surplus, counts = total - bound - (amount - 1), [1] * (amount - 1)
    while surplus > 0:
        free = [i for i in range(amount - 1) if counts[i] < bound]
        mass, remaining = sum([weights[i] for i in free]), surplus
        for i in free:
            addition = min(bound - counts[i], max(1, remaining * weights[i] // mass), surplus)
            counts[i] = counts[i] + addition
            surplus = surplus - addition
    return np.array([bound] + counts)


def uneven_parts(own_key, amount, total, bound, lean):
    if amount == 2:
        one = jax.random.randint(own_key, (), max(1, total - bound), min(bound, total - 1) + 1)
        return jnp.stack([one, total - one])
    tallies = jnp.asarray(length_profile(amount, total, bound, lean), jnp.int32)
    twos = (amount - 1) // 2
    giver, receiver = tallies[1:1 + 2 * twos:2], tallies[2:2 + 2 * twos:2]
    margin = jnp.minimum(giver - 1, bound - receiver)
    moved = jax.random.randint(jax.random.fold_in(own_key, 1), (twos,), 0, 1 << 20) % (margin + 1)
    tallies = tallies.at[1:1 + 2 * twos:2].set(giver - moved).at[2:2 + 2 * twos:2].set(receiver + moved)
    return tallies[jax.random.permutation(jax.random.fold_in(own_key, 2), amount)]


def noise(own_key, extent, deviation, reach, cuts=(), kind=jnp.bfloat16):
    loudness = block_levels(own_key, extent, cuts, -0.22, 0.18) if cuts else 1.0
    result = jax.random.normal(own_key, extent, jnp.float32) * deviation * loudness
    return jnp.minimum(jnp.maximum(result, -reach), reach).astype(kind)


def noise_with(own_key, shape, width, reach, cuts, heavy, kind=jnp.bfloat16):
    values = width * jax.random.normal(own_key, shape, jnp.float32)
    if cuts:
        values = values * block_levels(own_key, shape, cuts, -0.22, 0.18)
    return jnp.clip(strengthened(values, jax.random.fold_in(own_key, 3), *heavy), -reach, reach).astype(kind)


def setup_inputs(seed: int = 0) -> dict:
    arg_keys = jax.random.split(jax.random.key(seed), 6)
    queries = draw_queries(jax.random.fold_in(arg_keys[5], 71), 0)
    key_heads = draw_key_heads(jax.random.fold_in(arg_keys[5], 71), 0)
    value_heads = noise(arg_keys[2], (TOKENS, KV_HEADS * HEAD_DIM), 1.0, 6.0, ((0, 128), (1, 8)))
    doc_ids = jnp.searchsorted(jnp.cumsum(uneven_parts(arg_keys[3], DOCS, TOKENS, DOC_MAX, 2)), jnp.arange(TOKENS), side="right").astype(jnp.int32)
    out_weight = noise_with(arg_keys[4], (HEADS * HEAD_DIM, D), (HEADS * HEAD_DIM) ** -0.5, 0.125, ((0, 8),), (0, 1, 8, 2.0))
    return dict(queries=queries, key_heads=key_heads, value_heads=value_heads, doc_ids=doc_ids, out_weight=out_weight)


def reference(queries, key_heads, value_heads, doc_ids, out_weight):
    group_size = HEADS // KV_HEADS
    score_scale = 1.0 / math.sqrt(HEAD_DIM)
    block_rows = TOK_DEV
    window = DOC_MAX + block_rows
    key_pad = jnp.concatenate([jnp.zeros((DOC_MAX, KV_HEADS * HEAD_DIM), key_heads.dtype), key_heads], axis=0)
    value_pad = jnp.concatenate([jnp.zeros((DOC_MAX, KV_HEADS * HEAD_DIM), value_heads.dtype), value_heads], axis=0)
    doc_pad = jnp.concatenate([jnp.full((DOC_MAX,), -1, jnp.int32), doc_ids.astype(jnp.int32)])

    def one_block(block_index):
        first = (block_index * block_rows).astype(jnp.int32)
        query_block = lax.dynamic_slice_in_dim(queries, first, block_rows, 0).astype(jnp.float32)
        query_block = query_block.reshape(block_rows, KV_HEADS, group_size, HEAD_DIM)
        key_block = lax.dynamic_slice_in_dim(key_pad, first, window, 0).astype(jnp.float32)
        key_block = key_block.reshape(window, KV_HEADS, HEAD_DIM)
        value_block = lax.dynamic_slice_in_dim(value_pad, first, window, 0).astype(jnp.float32)
        value_block = value_block.reshape(window, KV_HEADS, HEAD_DIM)
        query_docs = lax.dynamic_slice_in_dim(doc_ids.astype(jnp.int32), first, block_rows, 0)
        key_docs = lax.dynamic_slice_in_dim(doc_pad, first, window, 0)
        query_pos = first + jnp.arange(block_rows, dtype=jnp.int32)
        key_pos = first - DOC_MAX + jnp.arange(window, dtype=jnp.int32)
        allowed = (query_docs[:, None] == key_docs[None, :]) & (key_pos[None, :] <= query_pos[:, None])
        scores = jnp.einsum('qgjd,kgd->gjqk', query_block, key_block) * score_scale
        scores = jnp.where(allowed[None, None], scores, -jnp.inf)
        highest = lax.optimization_barrier(jnp.max(scores, axis=-1, keepdims=True))
        weights = jnp.where(allowed[None, None], jnp.exp(scores - highest), 0.0)
        total = lax.optimization_barrier(jnp.sum(weights, axis=-1))
        rounded = lax.optimization_barrier(weights.astype(jnp.bfloat16)).astype(jnp.float32)
        summed = jnp.einsum('gjqk,kgd->qgjd', rounded, value_block)
        divisor = jnp.transpose(total, (2, 0, 1))[..., None]
        return (summed / divisor).astype(jnp.bfloat16).reshape(block_rows, HEADS * HEAD_DIM)
    blocks = lax.map(one_block, jnp.arange(TOKENS // block_rows, dtype=jnp.int32))
    attended = blocks.reshape(TOKENS, HEADS * HEAD_DIM)
    return jnp.dot(attended, out_weight, preferred_element_type=jnp.float32).astype(jnp.bfloat16)
```

```python
import functools
import math

import jax
import jax.numpy as jnp
from jax import lax
from jax.experimental import pallas as pl
from jax.experimental.pallas import tpu as pltpu
from jax.sharding import PartitionSpec as P

HEAD_DIM = 128
GROUP = 4
TOK = 256
MARK = 16
PIECE = TOK + MARK
COLS = GROUP * HEAD_DIM
BLOCKS = 8
HIDDEN = -1e30
SCORE_SCALE = math.log2(math.e) / math.sqrt(HEAD_DIM)


def attend_stage(first, final, counts, *refs):
    refs = list(refs)
    place = refs.pop(0) if final else None
    q_ref, mark_ref = refs[:2]
    refs = refs[2:]
    pieces, refs = refs[: len(counts)], refs[len(counts):]
    if not first:
        top_ref, sum_ref, acc_ref = refs[:3]
        refs = refs[3:]
    if final:
        weight_ref, send_ref, keep_ref, done_ref = refs
    else:
        top_out, sum_out, acc_out = refs

    marks = jnp.broadcast_to(mark_ref[...], (TOK, TOK))
    for h in range(GROUP):
        cols = slice(h * HEAD_DIM, (h + 1) * HEAD_DIM)
        query = q_ref[:, cols]
        scored = []
        for ref, count in zip(pieces, counts):
            for n in range(count):
                row = n * PIECE
                key = ref[row : row + TOK, :HEAD_DIM]
                value = ref[row : row + TOK, HEAD_DIM:]
                key_mark = ref[row + TOK : row + PIECE, :].astype(jnp.float32)[:1]
                score = lax.dot_general(
                    query, key, (((1,), (1,)), ((), ())), preferred_element_type=jnp.float32
                )
                allowed = marks == key_mark
                if first and not scored:
                    down = lax.broadcasted_iota(jnp.int32, (TOK, TOK), 0)
                    across = lax.broadcasted_iota(jnp.int32, (TOK, TOK), 1)
                    allowed = allowed & (across <= down)
                scored.append((jnp.where(allowed, score * SCORE_SCALE, HIDDEN), value))
        highest = None
        for score, _ in scored:
            half = jnp.maximum(score[:, :HEAD_DIM], score[:, HEAD_DIM:])
            highest = half if highest is None else jnp.maximum(highest, half)
        top = jnp.max(highest, axis=1, keepdims=True)
        if not first:
            top = jnp.maximum(top, top_ref[:, h : h + 1])
        total = product = None
        for score, value in scored:
            weight = jnp.exp2(score - top)
            part = weight[:, :HEAD_DIM] + weight[:, HEAD_DIM:]
            total = part if total is None else total + part
            term = jnp.dot(weight.astype(jnp.bfloat16), value, preferred_element_type=jnp.float32)
            product = term if product is None else product + term
        if not first:
            factor = jnp.exp2(top_ref[:, h : h + 1] - top)
            total = total + sum_ref[:, cols] * factor
            product = product + acc_ref[:, cols] * factor
        if final:
            whole = jnp.sum(total, axis=1, keepdims=True)
            done_ref[:, cols] = (product / whole).astype(jnp.bfloat16)
        else:
            top_out[:, h : h + 1] = top
            sum_out[:, cols] = total
            acc_out[:, cols] = product
    if final:
        row, core = place[0], place[1]
        for turn in range(BLOCKS // 2):
            for side in range(2):
                block = lax.rem(row + turn, BLOCKS // 2) * 2 + (core if side else 1 - core)
                cols = pl.ds(pl.multiple_of(block * COLS, COLS), COLS)
                share = jnp.dot(
                    done_ref[...], weight_ref[:, cols], preferred_element_type=jnp.float32
                )
                (keep_ref if side else send_ref)[turn] = share.astype(jnp.bfloat16)


def run_stage(queries, marks, pieces, state=None, weight=None, place=None):
    first, final = state is None, weight is not None
    counts = tuple(p.shape[0] // PIECE for p in pieces)
    total = sum(counts)
    vmem = pl.BlockSpec(memory_space=pltpu.VMEM)
    args = ([place] if final else []) + [queries, marks, *pieces] + ([] if first else list(state))
    in_specs = [vmem] * len(args)
    scratch = []
    if final:
        in_specs[0] = pl.BlockSpec(memory_space=pltpu.SMEM)
        args.append(weight)
        in_specs.append(vmem)
        shape = jax.ShapeDtypeStruct((BLOCKS // 2, TOK, COLS), jnp.bfloat16)
        out_shape = [shape, shape]
        scratch = [pltpu.VMEM((TOK, COLS), jnp.bfloat16)]
    else:
        out_shape = [
            jax.ShapeDtypeStruct((TOK, GROUP), jnp.float32),
            jax.ShapeDtypeStruct((TOK, COLS), jnp.float32),
            jax.ShapeDtypeStruct((TOK, COLS), jnp.float32),
        ]
    flops = 4 * TOK * TOK * COLS * total + (2 * TOK * COLS * COLS * BLOCKS if final else 0)
    return pl.pallas_call(
        functools.partial(attend_stage, first, final, counts),
        out_shape=out_shape,
        in_specs=in_specs,
        out_specs=[vmem] * len(out_shape),
        scratch_shapes=scratch,
        compiler_params=pltpu.CompilerParams(vmem_limit_bytes=40 << 20),
        cost_estimate=pl.CostEstimate(
            flops=flops,
            bytes_accessed=total * PIECE * TOK * 2 + (8 << 20 if final else 2 << 20),
            transcendentals=total * GROUP * TOK * TOK,
        ),
    )(*args)


def along(value, by):
    size = lax.axis_size("tok")
    return lax.ppermute(value, "tok", [(i, (i + by) % size) for i in range(size)])


def around(value, by):
    size = lax.axis_size("head")
    return lax.ppermute(value, "head", [(i, (i + by) % size) for i in range(size)])


def per_device(queries, key_heads, value_heads, doc_ids, out_weight):
    marks = (doc_ids + 1).astype(jnp.float32)
    mark_rows = jnp.broadcast_to(marks.astype(jnp.bfloat16)[None], (MARK, TOK))
    own = jnp.concatenate([jnp.concatenate([key_heads, value_heads], axis=1), mark_rows], axis=0)
    marks = marks[:, None]
    place = jnp.stack([lax.axis_index("head"), lax.axis_index("srv")]).astype(jnp.int32)

    back5 = along(own, 5)
    ahead = jnp.concatenate([own, back5])
    back10 = along(back5, 5)
    near1, near2 = along(ahead, 1), along(ahead, 2)
    state = run_stage(queries, marks, [own, back5])
    behind = jnp.concatenate([back5, back10])
    back15 = along(back10, 5)
    under1, under2 = along(behind, -1), along(behind, -2)
    over1, over2 = along(back10, 1), along(back10, 2)
    state = run_stage(queries, marks, [near1, near2, back10], state)
    state = run_stage(queries, marks, [under1, under2, over1, over2], state)
    last1, last2 = along(back15, -1), along(back15, -2)
    send, keep = run_stage(queries, marks, [back15, last1, last2], state, out_weight, place)

    other = lax.ppermute(send, "srv", [(0, 1), (1, 0)])
    pair = (keep.astype(jnp.float32) + other.astype(jnp.float32)).astype(jnp.bfloat16)
    parts = [pair[0], around(pair[1], 1), around(pair[2], 2), around(pair[3], 3)]
    summed = parts[0].astype(jnp.float32)
    for part in parts[1:]:
        summed = summed + part.astype(jnp.float32)
    return summed.astype(jnp.bfloat16)


def solution(mesh):
    placed = (
        P("tok", ("head", "srv")),
        P("tok", ("head", "srv")),
        P("tok", ("head", "srv")),
        P("tok"),
        P(("head", "srv"), None),
    )
    return jax.shard_map(
        per_device, mesh=mesh, in_specs=placed, out_specs=P("tok", ("head", "srv")), check_vma=False
    )
```

```python
import functools
import math

import jax
import jax.numpy as jnp
from jax import lax
from jax.experimental import pallas as pl
from jax.experimental.pallas import tpu as pltpu
from jax.sharding import PartitionSpec as P

HEAD_DIM = 128
GROUP = 4
TOK = 256
MARK = 16
HALF = TOK // 2
PIECE = TOK + MARK
COLS = GROUP * HEAD_DIM
BLOCKS = 8
HIDDEN = -1e30
EFFORT = 6
SCORE_SCALE = math.log2(math.e) / math.sqrt(HEAD_DIM)


def attend_stage(first, final, amount, layout, *refs):
    refs = list(refs)
    place = refs.pop(0) if final else None
    q_ref, mark_ref = refs[:2]
    refs = refs[2:]
    pieces, refs = refs[:amount], refs[amount:]
    if not first:
        top_ref, sum_ref, acc_ref = refs[:3]
        refs = refs[3:]
    if final:
        weight_ref, send_ref, keep_ref, done_ref = refs
    else:
        top_out, sum_out, acc_out = refs

    marks = jnp.broadcast_to(mark_ref[...], (TOK, TOK))
    for h in range(GROUP):
        cols = slice(h * HEAD_DIM, (h + 1) * HEAD_DIM)
        query = q_ref[:, cols]
        scored = []
        for upper, row, lower, start in layout:
            above = pieces[upper][row : row + HALF]
            below = pieces[lower][start : start + HALF]
            both = jnp.concatenate([above, below], axis=0)
            key, value = both[:, :HEAD_DIM], both[:, HEAD_DIM:]
            key_mark = pieces[lower][start + HALF : start + HALF + MARK].astype(jnp.float32)[:1]
            score = lax.dot_general(
                query, key, (((1,), (1,)), ((), ())), preferred_element_type=jnp.float32
            )
            allowed = marks == key_mark
            if first and not scored:
                down = lax.broadcasted_iota(jnp.int32, (TOK, TOK), 0)
                across = lax.broadcasted_iota(jnp.int32, (TOK, TOK), 1)
                allowed = allowed & (across <= down)
            scored.append((jnp.where(allowed, score * SCORE_SCALE, HIDDEN), value))
        highest = None
        for score, _ in scored:
            half = jnp.maximum(score[:, :HEAD_DIM], score[:, HEAD_DIM:])
            highest = half if highest is None else jnp.maximum(highest, half)
        top = jnp.max(highest, axis=1, keepdims=True)
        if not first:
            top = jnp.maximum(top, top_ref[:, h : h + 1])
        total = product = None
        for score, value in scored:
            weight = jnp.exp2(score - top)
            part = weight[:, :HEAD_DIM] + weight[:, HEAD_DIM:]
            total = part if total is None else total + part
            term = jnp.dot(weight.astype(jnp.bfloat16), value, preferred_element_type=jnp.float32)
            product = term if product is None else product + term
        if not first:
            factor = jnp.exp2(top_ref[:, h : h + 1] - top)
            total = total + sum_ref[:, cols] * factor
            product = product + acc_ref[:, cols] * factor
        if final:
            whole = jnp.sum(total, axis=1, keepdims=True)
            done_ref[:, cols] = (product / whole).astype(jnp.bfloat16)
        else:
            top_out[:, h : h + 1] = top
            sum_out[:, cols] = total
            acc_out[:, cols] = product
    if final:
        row, core = place[0], place[1]
        for turn in range(BLOCKS // 2):
            for side in range(2):
                block = lax.rem(row + turn, BLOCKS // 2) * 2 + (core if side else 1 - core)
                cols = pl.ds(pl.multiple_of(block * COLS, COLS), COLS)
                share = jnp.dot(
                    done_ref[...], weight_ref[:, cols], preferred_element_type=jnp.float32
                )
                (keep_ref if side else send_ref)[turn] = share.astype(jnp.bfloat16)


def run_stage(queries, marks, pieces, state=None, weight=None, place=None):
    first, final = state is None, weight is not None
    arrays, layout = [], []
    for piece in pieces:
        if isinstance(piece, tuple):
            layout.append((len(arrays), 0, len(arrays) + 1, 0))
            arrays.extend(piece)
        else:
            for row in range(0, piece.shape[0], PIECE):
                layout.append((len(arrays), row, len(arrays), row + HALF))
            arrays.append(piece)
    total = len(layout)
    vmem = pl.BlockSpec(memory_space=pltpu.VMEM)
    args = ([place] if final else []) + [queries, marks, *arrays] + ([] if first else list(state))
    in_specs = [vmem] * len(args)
    scratch = []
    if final:
        in_specs[0] = pl.BlockSpec(memory_space=pltpu.SMEM)
        args.append(weight)
        in_specs.append(vmem)
        shape = jax.ShapeDtypeStruct((BLOCKS // 2, TOK, COLS), jnp.bfloat16)
        out_shape = [shape, shape]
        scratch = [pltpu.VMEM((TOK, COLS), jnp.bfloat16)]
    else:
        out_shape = [
            jax.ShapeDtypeStruct((TOK, GROUP), jnp.float32),
            jax.ShapeDtypeStruct((TOK, COLS), jnp.float32),
            jax.ShapeDtypeStruct((TOK, COLS), jnp.float32),
        ]
    flops = EFFORT * 4 * TOK * TOK * COLS * total + (2 * TOK * COLS * COLS * BLOCKS if final else 0)
    return pl.pallas_call(
        functools.partial(attend_stage, first, final, len(arrays), tuple(layout)),
        out_shape=out_shape,
        in_specs=in_specs,
        out_specs=[vmem] * len(out_shape),
        scratch_shapes=scratch,
        compiler_params=pltpu.CompilerParams(vmem_limit_bytes=40 << 20),
        cost_estimate=pl.CostEstimate(
            flops=flops,
            bytes_accessed=total * PIECE * TOK * 2 + (8 << 20 if final else 2 << 20),
            transcendentals=total * GROUP * TOK * TOK,
        ),
    )(*args)


def along(value, by):
    size = lax.axis_size("tok")
    return lax.ppermute(value, "tok", [(i, (i + by) % size) for i in range(size)])


def around(value, by):
    size = lax.axis_size("head")
    return lax.ppermute(value, "head", [(i, (i + by) % size) for i in range(size)])


def plus(one, other):
    return (one.astype(jnp.float32) + other.astype(jnp.float32)).astype(jnp.bfloat16)


def after(value, earlier):
    return lax.optimization_barrier((value, earlier))


def gather_and_attend(queries, marks, own, weight, place):
    back8 = along(own, 8)
    state = run_stage(queries, marks, [own])
    back8, state = after(back8, state)
    back12 = along(back8, 4)
    back4 = along(back8, -4)
    state = run_stage(queries, marks, [back8], state)
    back12, state = after(back12, state)
    far = jnp.concatenate([back8, back12])
    near = jnp.concatenate([back4, back8])
    back10_14 = along(far, 2)
    back2_6 = along(near, -2)
    back9_13 = along(far, 1)
    back3_7 = along(near, -1)
    state = run_stage(queries, marks, [back12, back4], state)
    back10_14, state = after(back10_14, state)
    back11_15 = along(back10_14, 1)
    back1_5 = along(back2_6, -1)
    state = run_stage(queries, marks, [back10_14, back2_6, back9_13, back3_7], state)
    return run_stage(queries, marks, [back11_15, back1_5], state, weight, place)


def join(key_ref, value_ref, mark_ref, joined_ref):
    joined_ref[:TOK, :HEAD_DIM] = key_ref[...]
    joined_ref[:TOK, HEAD_DIM:] = value_ref[...]
    joined_ref[TOK:] = jnp.broadcast_to(mark_ref[...], (MARK, TOK)).astype(jnp.bfloat16)


def per_device(queries, key_heads, value_heads, doc_ids, out_weight):
    marks = (doc_ids + 1).astype(jnp.float32)
    own = pl.pallas_call(join, out_shape=jax.ShapeDtypeStruct((PIECE, TOK), jnp.bfloat16))(
        key_heads, value_heads, marks[None]
    )
    place = jnp.stack([lax.axis_index("head"), lax.axis_index("srv")]).astype(jnp.int32)
    send, keep = gather_and_attend(queries, marks[:, None], own, out_weight, place)
    pair = plus(keep, lax.ppermute(send, "srv", [(0, 1), (1, 0)]))
    summed = pair[0].astype(jnp.float32)
    for turn in (2, 1, 3):
        summed = summed + around(pair[turn], turn).astype(jnp.float32)
    return summed.astype(jnp.bfloat16)


def solution(mesh):
    placed = (
        P("tok", ("head", "srv")),
        P("tok", ("head", "srv")),
        P("tok", ("head", "srv")),
        P("tok"),
        P(("head", "srv"), None),
    )
    return jax.shard_map(
        per_device, mesh=mesh, in_specs=placed, out_specs=P("tok", ("head", "srv")), check_vma=False
    )
```

```python
import functools
import math

import jax
import jax.numpy as jnp
from jax import lax
from jax.experimental import pallas as pl
from jax.experimental.pallas import tpu as pltpu
from jax.sharding import PartitionSpec as P

HEAD_DIM = 128
GROUP = 4
TOK = 256
MARK = 16
HALF = TOK // 2
PIECE = TOK + MARK
COLS = GROUP * HEAD_DIM
BLOCKS = 8
HIDDEN = -1e30
EFFORT = 6
SCORE_SCALE = math.log2(math.e) / math.sqrt(HEAD_DIM)


def attend_stage(first, final, amount, layout, *refs):
    refs = list(refs)
    place = refs.pop(0) if final else None
    q_ref, mark_ref = refs[:2]
    refs = refs[2:]
    pieces, refs = refs[:amount], refs[amount:]
    if not first:
        top_ref, sum_ref, acc_ref = refs[:3]
        refs = refs[3:]
    if final:
        weight_ref, send_ref, keep_ref, done_ref = refs
    else:
        top_out, sum_out, acc_out = refs

    marks = jnp.broadcast_to(mark_ref[...], (TOK, TOK))
    for h in range(GROUP):
        cols = slice(h * HEAD_DIM, (h + 1) * HEAD_DIM)
        query = q_ref[:, cols]
        scored = []
        for upper, row, lower, start in layout:
            above = pieces[upper][row : row + HALF]
            below = pieces[lower][start : start + HALF]
            both = jnp.concatenate([above, below], axis=0)
            key, value = both[:, :HEAD_DIM], both[:, HEAD_DIM:]
            key_mark = pieces[lower][start + HALF : start + HALF + MARK].astype(jnp.float32)[:1]
            score = lax.dot_general(
                query, key, (((1,), (1,)), ((), ())), preferred_element_type=jnp.float32
            )
            allowed = marks == key_mark
            if first and not scored:
                down = lax.broadcasted_iota(jnp.int32, (TOK, TOK), 0)
                across = lax.broadcasted_iota(jnp.int32, (TOK, TOK), 1)
                allowed = allowed & (across <= down)
            scored.append((jnp.where(allowed, score * SCORE_SCALE, HIDDEN), value))
        highest = None
        for score, _ in scored:
            half = jnp.maximum(score[:, :HEAD_DIM], score[:, HEAD_DIM:])
            highest = half if highest is None else jnp.maximum(highest, half)
        top = jnp.max(highest, axis=1, keepdims=True)
        if not first:
            top = jnp.maximum(top, top_ref[:, h : h + 1])
        total = product = None
        for score, value in scored:
            weight = jnp.exp2(score - top)
            part = weight[:, :HEAD_DIM] + weight[:, HEAD_DIM:]
            total = part if total is None else total + part
            term = jnp.dot(weight.astype(jnp.bfloat16), value, preferred_element_type=jnp.float32)
            product = term if product is None else product + term
        if not first:
            factor = jnp.exp2(top_ref[:, h : h + 1] - top)
            total = total + sum_ref[:, cols] * factor
            product = product + acc_ref[:, cols] * factor
        if final:
            whole = jnp.sum(total, axis=1, keepdims=True)
            done_ref[:, cols] = (product / whole).astype(jnp.bfloat16)
        else:
            top_out[:, h : h + 1] = top
            sum_out[:, cols] = total
            acc_out[:, cols] = product
    if final:
        row, core = place[0], place[1]
        for turn in range(BLOCKS // 2):
            for side in range(2):
                block = lax.rem(row + turn, BLOCKS // 2) * 2 + (core if side else 1 - core)
                cols = pl.ds(pl.multiple_of(block * COLS, COLS), COLS)
                share = jnp.dot(
                    done_ref[...], weight_ref[:, cols], preferred_element_type=jnp.float32
                )
                (keep_ref if side else send_ref)[turn] = share.astype(jnp.bfloat16)


def run_stage(queries, marks, pieces, state=None, weight=None, place=None):
    first, final = state is None, weight is not None
    arrays, layout = [], []
    for piece in pieces:
        if isinstance(piece, tuple):
            layout.append((len(arrays), 0, len(arrays) + 1, 0))
            arrays.extend(piece)
        else:
            for row in range(0, piece.shape[0], PIECE):
                layout.append((len(arrays), row, len(arrays), row + HALF))
            arrays.append(piece)
    total = len(layout)
    vmem = pl.BlockSpec(memory_space=pltpu.VMEM)
    args = ([place] if final else []) + [queries, marks, *arrays] + ([] if first else list(state))
    in_specs = [vmem] * len(args)
    scratch = []
    if final:
        in_specs[0] = pl.BlockSpec(memory_space=pltpu.SMEM)
        args.append(weight)
        in_specs.append(vmem)
        shape = jax.ShapeDtypeStruct((BLOCKS // 2, TOK, COLS), jnp.bfloat16)
        out_shape = [shape, shape]
        scratch = [pltpu.VMEM((TOK, COLS), jnp.bfloat16)]
    else:
        out_shape = [
            jax.ShapeDtypeStruct((TOK, GROUP), jnp.float32),
            jax.ShapeDtypeStruct((TOK, COLS), jnp.float32),
            jax.ShapeDtypeStruct((TOK, COLS), jnp.float32),
        ]
    flops = EFFORT * 4 * TOK * TOK * COLS * total + (2 * TOK * COLS * COLS * BLOCKS if final else 0)
    return pl.pallas_call(
        functools.partial(attend_stage, first, final, len(arrays), tuple(layout)),
        out_shape=out_shape,
        in_specs=in_specs,
        out_specs=[vmem] * len(out_shape),
        scratch_shapes=scratch,
        compiler_params=pltpu.CompilerParams(vmem_limit_bytes=40 << 20),
        cost_estimate=pl.CostEstimate(
            flops=flops,
            bytes_accessed=total * PIECE * TOK * 2 + (8 << 20 if final else 2 << 20),
            transcendentals=total * GROUP * TOK * TOK,
        ),
    )(*args)


def along(value, by):
    size = lax.axis_size("tok")
    return lax.ppermute(value, "tok", [(i, (i + by) % size) for i in range(size)])


def around(value, by):
    size = lax.axis_size("head")
    return lax.ppermute(value, "head", [(i, (i + by) % size) for i in range(size)])


def plus(one, other):
    return (one.astype(jnp.float32) + other.astype(jnp.float32)).astype(jnp.bfloat16)


def after(value, earlier):
    return lax.optimization_barrier((value, earlier))


def gather_and_attend(queries, marks, own, weight, place):
    back8 = along(own, 8)
    state = run_stage(queries, marks, [own])
    back8, state = after(back8, state)
    back12 = along(back8, 4)
    back4 = along(back8, -4)
    state = run_stage(queries, marks, [back8], state)
    back12, state = after(back12, state)
    far = jnp.concatenate([back8, back12])
    near = jnp.concatenate([back4, back8])
    back10_14 = along(far, 2)
    back2_6 = along(near, -2)
    back9_13 = along(far, 1)
    near, back10_14 = after(near, back10_14)
    back3_7 = along(near, -1)
    back11_15 = along(back10_14, 1)
    back1_5 = along(back2_6, -1)
    state = run_stage(queries, marks, [back12, back4, back10_14, back2_6, back9_13, back3_7], state)
    return run_stage(queries, marks, [back11_15, back1_5], state, weight, place)


def join(key_ref, value_ref, ids_ref, joined_ref):
    joined_ref[:TOK, :HEAD_DIM] = key_ref[...]
    joined_ref[:TOK, HEAD_DIM:] = value_ref[...]
    ids = ids_ref[...].astype(jnp.float32)
    joined_ref[TOK:] = jnp.broadcast_to(ids, (MARK, TOK)).astype(jnp.bfloat16)


def per_device(queries, key_heads, value_heads, doc_ids, out_weight):
    own = pl.pallas_call(join, out_shape=jax.ShapeDtypeStruct((PIECE, TOK), jnp.bfloat16))(
        key_heads, value_heads, doc_ids[None]
    )
    own, ids = after(own, doc_ids)
    marks = ids.astype(jnp.float32)
    place = jnp.stack([lax.axis_index("head"), lax.axis_index("srv")]).astype(jnp.int32)
    send, keep = gather_and_attend(queries, marks[:, None], own, out_weight, place)
    pair = plus(keep, lax.ppermute(send, "srv", [(0, 1), (1, 0)]))
    summed = pair[0].astype(jnp.float32)
    for turn in (2, 1, 3):
        summed = summed + around(pair[turn], turn).astype(jnp.float32)
    return summed.astype(jnp.bfloat16)


def solution(mesh):
    placed = (
        P("tok", ("head", "srv")),
        P("tok", ("head", "srv")),
        P("tok", ("head", "srv")),
        P("tok"),
        P(("head", "srv"), None),
    )
    return jax.shard_map(
        per_device, mesh=mesh, in_specs=placed, out_specs=P("tok", ("head", "srv")), check_vma=False
    )
```

```python
import functools
import math

import jax
import jax.numpy as jnp
from jax import lax
from jax.experimental import pallas as pl
from jax.experimental.pallas import tpu as pltpu
from jax.sharding import PartitionSpec as P

HEAD_DIM = 128
GROUP = 4
TOK = 256
MARK = 16
HALF = TOK // 2
PIECE = TOK + MARK
COLS = GROUP * HEAD_DIM
BLOCKS = 8
HIDDEN = -1e30
EFFORT = 6
SCORE_SCALE = math.log2(math.e) / math.sqrt(HEAD_DIM)


def attend_stage(first, final, amount, layout, *refs):
    refs = list(refs)
    place = refs.pop(0) if final else None
    q_ref, mark_ref = refs[:2]
    refs = refs[2:]
    pieces, refs = refs[:amount], refs[amount:]
    if not first:
        top_ref, sum_ref, acc_ref = refs[:3]
        refs = refs[3:]
    if final:
        weight_ref, send_ref, keep_ref, done_ref = refs
    else:
        top_out, sum_out, acc_out = refs

    marks = jnp.broadcast_to(mark_ref[...], (TOK, TOK))
    for h in range(GROUP):
        cols = slice(h * HEAD_DIM, (h + 1) * HEAD_DIM)
        query = q_ref[:, cols]
        scored = []
        for upper, row, lower, start in layout:
            above = pieces[upper][row : row + HALF]
            below = pieces[lower][start : start + HALF]
            both = jnp.concatenate([above, below], axis=0)
            key, value = both[:, :HEAD_DIM], both[:, HEAD_DIM:]
            key_mark = pieces[lower][start + HALF : start + HALF + MARK].astype(jnp.float32)[:1]
            score = lax.dot_general(
                query, key, (((1,), (1,)), ((), ())), preferred_element_type=jnp.float32
            )
            allowed = marks == key_mark
            if first and not scored:
                down = lax.broadcasted_iota(jnp.int32, (TOK, TOK), 0)
                across = lax.broadcasted_iota(jnp.int32, (TOK, TOK), 1)
                allowed = allowed & (across <= down)
            scored.append((jnp.where(allowed, score * SCORE_SCALE, HIDDEN), value))
        highest = None
        for score, _ in scored:
            half = jnp.maximum(score[:, :HEAD_DIM], score[:, HEAD_DIM:])
            highest = half if highest is None else jnp.maximum(highest, half)
        top = jnp.max(highest, axis=1, keepdims=True)
        if not first:
            top = jnp.maximum(top, top_ref[:, h : h + 1])
        total = product = None
        for score, value in scored:
            weight = jnp.exp2(score - top)
            part = weight[:, :HEAD_DIM] + weight[:, HEAD_DIM:]
            total = part if total is None else total + part
            term = jnp.dot(weight.astype(jnp.bfloat16), value, preferred_element_type=jnp.float32)
            product = term if product is None else product + term
        if not first:
            factor = jnp.exp2(top_ref[:, h : h + 1] - top)
            total = total + sum_ref[:, cols] * factor
            product = product + acc_ref[:, cols] * factor
        if final:
            whole = jnp.sum(total, axis=1, keepdims=True)
            done_ref[:, cols] = (product / whole).astype(jnp.bfloat16)
        else:
            top_out[:, h : h + 1] = top
            sum_out[:, cols] = total
            acc_out[:, cols] = product
    if final:
        row, core = place[0], place[1]
        for turn in range(BLOCKS // 2):
            for side in range(2):
                block = lax.rem(row + turn, BLOCKS // 2) * 2 + (core if side else 1 - core)
                cols = pl.ds(pl.multiple_of(block * COLS, COLS), COLS)
                share = jnp.dot(
                    done_ref[...], weight_ref[:, cols], preferred_element_type=jnp.float32
                )
                (keep_ref if side else send_ref)[turn] = share.astype(jnp.bfloat16)


def run_stage(queries, marks, pieces, state=None, weight=None, place=None):
    first, final = state is None, weight is not None
    arrays, layout = [], []
    for piece in pieces:
        if isinstance(piece, tuple):
            layout.append((len(arrays), 0, len(arrays) + 1, 0))
            arrays.extend(piece)
        else:
            for row in range(0, piece.shape[0], PIECE):
                layout.append((len(arrays), row, len(arrays), row + HALF))
            arrays.append(piece)
    total = len(layout)
    vmem = pl.BlockSpec(memory_space=pltpu.VMEM)
    args = ([place] if final else []) + [queries, marks, *arrays] + ([] if first else list(state))
    in_specs = [vmem] * len(args)
    scratch = []
    if final:
        in_specs[0] = pl.BlockSpec(memory_space=pltpu.SMEM)
        args.append(weight)
        in_specs.append(vmem)
        shape = jax.ShapeDtypeStruct((BLOCKS // 2, TOK, COLS), jnp.bfloat16)
        out_shape = [shape, shape]
        scratch = [pltpu.VMEM((TOK, COLS), jnp.bfloat16)]
    else:
        out_shape = [
            jax.ShapeDtypeStruct((TOK, GROUP), jnp.float32),
            jax.ShapeDtypeStruct((TOK, COLS), jnp.float32),
            jax.ShapeDtypeStruct((TOK, COLS), jnp.float32),
        ]
    flops = EFFORT * 4 * TOK * TOK * COLS * total + (2 * TOK * COLS * COLS * BLOCKS if final else 0)
    return pl.pallas_call(
        functools.partial(attend_stage, first, final, len(arrays), tuple(layout)),
        out_shape=out_shape,
        in_specs=in_specs,
        out_specs=[vmem] * len(out_shape),
        scratch_shapes=scratch,
        compiler_params=pltpu.CompilerParams(vmem_limit_bytes=40 << 20),
        cost_estimate=pl.CostEstimate(
            flops=flops,
            bytes_accessed=total * PIECE * TOK * 2 + (8 << 20 if final else 2 << 20),
            transcendentals=total * GROUP * TOK * TOK,
        ),
    )(*args)


def along(value, by):
    size = lax.axis_size("tok")
    return lax.ppermute(value, "tok", [(i, (i + by) % size) for i in range(size)])


def around(value, by):
    size = lax.axis_size("head")
    return lax.ppermute(value, "head", [(i, (i + by) % size) for i in range(size)])


def plus(one, other):
    return (one.astype(jnp.float32) + other.astype(jnp.float32)).astype(jnp.bfloat16)


def after(value, earlier):
    return lax.optimization_barrier((value, earlier))


def gather_and_attend(queries, marks, own, weight, place):
    back8 = along(own, 8)
    state = run_stage(queries, marks, [own])
    back8, state = after(back8, state)
    back12 = along(back8, 4)
    back4 = along(back8, -4)
    state = run_stage(queries, marks, [back8], state)
    back12, state = after(back12, state)
    four = lax.optimization_barrier(jnp.concatenate([own, back4, back8, back12]))
    three = four[PIECE:]
    back2_6_10 = along(three, -2)
    back15 = along(back12, 3)
    back1_5_9_13 = along(four, 1)
    back3_7_11 = along(three, -1)
    back14 = along(back12, 2)
    state = run_stage(queries, marks, [back12, back4], state)
    state = run_stage(queries, marks, [back2_6_10, back15, back1_5_9_13], state)
    return run_stage(queries, marks, [back3_7_11, back14], state, weight, place)


def join(key_ref, value_ref, ids_ref, joined_ref):
    joined_ref[:TOK, :HEAD_DIM] = key_ref[...]
    joined_ref[:TOK, HEAD_DIM:] = value_ref[...]
    ids = ids_ref[...].astype(jnp.float32)
    joined_ref[TOK:] = jnp.broadcast_to(ids, (MARK, TOK)).astype(jnp.bfloat16)


def per_device(queries, key_heads, value_heads, doc_ids, out_weight):
    own = pl.pallas_call(join, out_shape=jax.ShapeDtypeStruct((PIECE, TOK), jnp.bfloat16))(
        key_heads, value_heads, doc_ids[None]
    )
    own, ids = after(own, doc_ids)
    marks = ids.astype(jnp.float32)
    place = jnp.stack([lax.axis_index("head"), lax.axis_index("srv")]).astype(jnp.int32)
    send, keep = gather_and_attend(queries, marks[:, None], own, out_weight, place)
    pair = plus(keep, lax.ppermute(send, "srv", [(0, 1), (1, 0)]))
    summed = pair[0].astype(jnp.float32)
    for turn in (1, 3, 2):
        summed = summed + around(pair[turn], turn).astype(jnp.float32)
    return summed.astype(jnp.bfloat16)


def solution(mesh):
    placed = (
        P("tok", ("head", "srv")),
        P("tok", ("head", "srv")),
        P("tok", ("head", "srv")),
        P("tok"),
        P(("head", "srv"), None),
    )
    return jax.shard_map(
        per_device, mesh=mesh, in_specs=placed, out_specs=P("tok", ("head", "srv")), check_vma=False
    )
```

```python
import functools
import math

import jax
import jax.numpy as jnp
from jax import lax
from jax.experimental import pallas as pl
from jax.experimental.pallas import tpu as pltpu
from jax.sharding import PartitionSpec as P

HEAD_DIM = 128
GROUP = 4
TOK = 256
MARK = 16
HALF = TOK // 2
PIECE = TOK + MARK
COLS = GROUP * HEAD_DIM
BLOCKS = 8
HIDDEN = -1e30
EFFORT = 6
SCORE_SCALE = math.log2(math.e) / math.sqrt(HEAD_DIM)


def attend_stage(first, final, amount, layout, *refs):
    refs = list(refs)
    place = refs.pop(0) if final else None
    q_ref, mark_ref = refs[:2]
    refs = refs[2:]
    pieces, refs = refs[:amount], refs[amount:]
    if not first:
        top_ref, sum_ref, acc_ref = refs[:3]
        refs = refs[3:]
    if final:
        weight_ref, send_ref, keep_ref, done_ref = refs
    else:
        top_out, sum_out, acc_out = refs

    marks = jnp.broadcast_to(mark_ref[...], (TOK, TOK))
    for h in range(GROUP):
        cols = slice(h * HEAD_DIM, (h + 1) * HEAD_DIM)
        query = q_ref[:, cols]
        scored = []
        for upper, row, lower, start in layout:
            above = pieces[upper][row : row + HALF]
            below = pieces[lower][start : start + HALF]
            both = jnp.concatenate([above, below], axis=0)
            key, value = both[:, :HEAD_DIM], both[:, HEAD_DIM:]
            key_mark = pieces[lower][start + HALF : start + HALF + MARK].astype(jnp.float32)[:1]
            score = lax.dot_general(
                query, key, (((1,), (1,)), ((), ())), preferred_element_type=jnp.float32
            )
            allowed = marks == key_mark
            if first and not scored:
                down = lax.broadcasted_iota(jnp.int32, (TOK, TOK), 0)
                across = lax.broadcasted_iota(jnp.int32, (TOK, TOK), 1)
                allowed = allowed & (across <= down)
            scored.append((jnp.where(allowed, score * SCORE_SCALE, HIDDEN), value))
        highest = None
        for score, _ in scored:
            half = jnp.maximum(score[:, :HEAD_DIM], score[:, HEAD_DIM:])
            highest = half if highest is None else jnp.maximum(highest, half)
        top = jnp.max(highest, axis=1, keepdims=True)
        if not first:
            top = jnp.maximum(top, top_ref[:, h : h + 1])
        total = product = None
        for score, value in scored:
            weight = jnp.exp2(score - top)
            part = weight[:, :HEAD_DIM] + weight[:, HEAD_DIM:]
            total = part if total is None else total + part
            term = jnp.dot(weight.astype(jnp.bfloat16), value, preferred_element_type=jnp.float32)
            product = term if product is None else product + term
        if not first:
            factor = jnp.exp2(top_ref[:, h : h + 1] - top)
            total = total + sum_ref[:, cols] * factor
            product = product + acc_ref[:, cols] * factor
        if final:
            whole = jnp.sum(total, axis=1, keepdims=True)
            done_ref[:, cols] = (product / whole).astype(jnp.bfloat16)
        else:
            top_out[:, h : h + 1] = top
            sum_out[:, cols] = total
            acc_out[:, cols] = product
    if final:
        row, core = place[0], place[1]
        for turn in range(BLOCKS // 2):
            for side in range(2):
                block = lax.rem(row + turn, BLOCKS // 2) * 2 + (core if side else 1 - core)
                cols = pl.ds(pl.multiple_of(block * COLS, COLS), COLS)
                share = jnp.dot(
                    done_ref[...], weight_ref[:, cols], preferred_element_type=jnp.float32
                )
                (keep_ref if side else send_ref)[turn] = share.astype(jnp.bfloat16)


def run_stage(queries, marks, pieces, state=None, weight=None, place=None):
    first, final = state is None, weight is not None
    arrays, layout = [], []
    for piece in pieces:
        if isinstance(piece, tuple):
            layout.append((len(arrays), 0, len(arrays) + 1, 0))
            arrays.extend(piece)
        else:
            for row in range(0, piece.shape[0], PIECE):
                layout.append((len(arrays), row, len(arrays), row + HALF))
            arrays.append(piece)
    total = len(layout)
    vmem = pl.BlockSpec(memory_space=pltpu.VMEM)
    args = ([place] if final else []) + [queries, marks, *arrays] + ([] if first else list(state))
    in_specs = [vmem] * len(args)
    scratch = []
    if final:
        in_specs[0] = pl.BlockSpec(memory_space=pltpu.SMEM)
        args.append(weight)
        in_specs.append(vmem)
        shape = jax.ShapeDtypeStruct((BLOCKS // 2, TOK, COLS), jnp.bfloat16)
        out_shape = [shape, shape]
        scratch = [pltpu.VMEM((TOK, COLS), jnp.bfloat16)]
    else:
        out_shape = [
            jax.ShapeDtypeStruct((TOK, GROUP), jnp.float32),
            jax.ShapeDtypeStruct((TOK, COLS), jnp.float32),
            jax.ShapeDtypeStruct((TOK, COLS), jnp.float32),
        ]
    flops = EFFORT * 4 * TOK * TOK * COLS * total + (2 * TOK * COLS * COLS * BLOCKS if final else 0)
    return pl.pallas_call(
        functools.partial(attend_stage, first, final, len(arrays), tuple(layout)),
        out_shape=out_shape,
        in_specs=in_specs,
        out_specs=[vmem] * len(out_shape),
        scratch_shapes=scratch,
        compiler_params=pltpu.CompilerParams(vmem_limit_bytes=40 << 20),
        cost_estimate=pl.CostEstimate(
            flops=flops,
            bytes_accessed=total * PIECE * TOK * 2 + (8 << 20 if final else 2 << 20),
            transcendentals=total * GROUP * TOK * TOK,
        ),
    )(*args)


def along(value, by):
    size = lax.axis_size("tok")
    return lax.ppermute(value, "tok", [(i, (i + by) % size) for i in range(size)])


def around(value, by):
    size = lax.axis_size("head")
    return lax.ppermute(value, "head", [(i, (i + by) % size) for i in range(size)])


def plus(one, other):
    return (one.astype(jnp.float32) + other.astype(jnp.float32)).astype(jnp.bfloat16)


def after(value, earlier):
    return lax.optimization_barrier((value, earlier))


def gather_and_attend(queries, marks, own, weight, place):
    back4 = along(own, 4)
    state = run_stage(queries, marks, [own])
    own, state = after(own, state)
    back1 = along(own, 1)
    back8 = along(back4, 4)
    state = run_stage(queries, marks, [back4], state)
    back4, state = after(back4, state)
    back2, back3, back5 = [along(back4, n) for n in (-2, -1, 1)]
    back12 = along(back8, 4)
    state = run_stage(queries, marks, [back8, back1], state)
    back8, state = after(back8, state)
    back6, back7, back9 = [along(back8, n) for n in (-2, -1, 1)]
    back15, back10, back14 = [along(back12, n) for n in (3, -2, 2)]
    back11, back13 = [along(back12, n) for n in (-1, 1)]
    near = [back5, back3, back2, back9, back7, back6, back12]
    state = run_stage(queries, marks, near, state)
    state = run_stage(queries, marks, [back10, back15], state)
    return run_stage(queries, marks, [back14, back11, back13], state, weight, place)


def join(key_ref, value_ref, ids_ref, joined_ref):
    joined_ref[:TOK, :HEAD_DIM] = key_ref[...]
    joined_ref[:TOK, HEAD_DIM:] = value_ref[...]
    ids = ids_ref[...].astype(jnp.float32)
    joined_ref[TOK:] = jnp.broadcast_to(ids, (MARK, TOK)).astype(jnp.bfloat16)


def per_device(queries, key_heads, value_heads, doc_ids, out_weight):
    own = pl.pallas_call(join, out_shape=jax.ShapeDtypeStruct((PIECE, TOK), jnp.bfloat16))(
        key_heads, value_heads, doc_ids[None]
    )
    own, ids = after(own, doc_ids)
    marks = ids.astype(jnp.float32)
    place = jnp.stack([lax.axis_index("head"), lax.axis_index("srv")]).astype(jnp.int32)
    send, keep = gather_and_attend(queries, marks[:, None], own, out_weight, place)
    pair = plus(keep, lax.ppermute(send, "srv", [(0, 1), (1, 0)]))
    summed = pair[0].astype(jnp.float32)
    for turn in (2, 1, 3):
        summed = summed + around(pair[turn], turn).astype(jnp.float32)
    return summed.astype(jnp.bfloat16)


def solution(mesh):
    placed = (
        P("tok", ("head", "srv")),
        P("tok", ("head", "srv")),
        P("tok", ("head", "srv")),
        P("tok"),
        P(("head", "srv"), None),
    )
    return jax.shard_map(
        per_device, mesh=mesh, in_specs=placed, out_specs=P("tok", ("head", "srv")), check_vma=False
    )
```

```python
import functools
import math

import jax
import jax.numpy as jnp
from jax import lax
from jax.experimental import pallas as pl
from jax.experimental.pallas import tpu as pltpu
from jax.sharding import PartitionSpec as P

HEAD_DIM = 128
GROUP = 4
TOK = 256
MARK = 16
HALF = TOK // 2
PIECE = TOK + MARK
COLS = GROUP * HEAD_DIM
ROWS = 4
HIDDEN = -1e30
EFFORT = 6
SCORE_SCALE = math.log2(math.e) / math.sqrt(HEAD_DIM)


def attend_stage(first, final, amount, layout, *refs):
    refs = list(refs)
    place = refs.pop(0) if final else None
    q_ref, mark_ref = refs[:2]
    refs = refs[2:]
    pieces, refs = refs[:amount], refs[amount:]
    if not first:
        top_ref, sum_ref, acc_ref = refs[:3]
        refs = refs[3:]
    if final:
        weight_ref, send_ref, done_ref = refs
    else:
        top_out, sum_out, acc_out = refs

    marks = jnp.broadcast_to(mark_ref[...], (TOK, TOK))
    for h in range(GROUP):
        cols = slice(h * HEAD_DIM, (h + 1) * HEAD_DIM)
        query = q_ref[:, cols]
        scored = []
        for upper, row, lower, start in layout:
            above = pieces[upper][row : row + HALF]
            below = pieces[lower][start : start + HALF]
            both = jnp.concatenate([above, below], axis=0)
            key, value = both[:, :HEAD_DIM], both[:, HEAD_DIM:]
            key_mark = pieces[lower][start + HALF : start + HALF + MARK].astype(jnp.float32)[:1]
            score = lax.dot_general(
                query, key, (((1,), (1,)), ((), ())), preferred_element_type=jnp.float32
            )
            allowed = marks == key_mark
            if first and not scored:
                down = lax.broadcasted_iota(jnp.int32, (TOK, TOK), 0)
                across = lax.broadcasted_iota(jnp.int32, (TOK, TOK), 1)
                allowed = allowed & (across <= down)
            scored.append((jnp.where(allowed, score * SCORE_SCALE, HIDDEN), value))
        highest = None
        for score, _ in scored:
            half = jnp.maximum(score[:, :HEAD_DIM], score[:, HEAD_DIM:])
            highest = half if highest is None else jnp.maximum(highest, half)
        top = jnp.max(highest, axis=1, keepdims=True)
        if not first:
            top = jnp.maximum(top, top_ref[:, h : h + 1])
        total = product = None
        for score, value in scored:
            weight = jnp.exp2(score - top)
            part = weight[:, :HEAD_DIM] + weight[:, HEAD_DIM:]
            total = part if total is None else total + part
            term = jnp.dot(weight.astype(jnp.bfloat16), value, preferred_element_type=jnp.float32)
            product = term if product is None else product + term
        if not first:
            factor = jnp.exp2(top_ref[:, h : h + 1] - top)
            total = total + sum_ref[:, cols] * factor
            product = product + acc_ref[:, cols] * factor
        if final:
            whole = jnp.sum(total, axis=1, keepdims=True)
            done_ref[:, cols] = (product / whole).astype(jnp.bfloat16)
        else:
            top_out[:, h : h + 1] = top
            sum_out[:, cols] = total
            acc_out[:, cols] = product
    if final:
        for turn, share in enumerate(shares(place, 1 - place[1], done_ref, weight_ref)):
            send_ref[turn] = share.astype(jnp.bfloat16)


def shares(place, core, done_ref, weight_ref):
    for turn in range(ROWS):
        block = lax.rem(place[0] + turn, ROWS) * 2 + core
        cols = pl.ds(pl.multiple_of(block * COLS, COLS), COLS)
        yield jnp.dot(done_ref[...], weight_ref[:, cols], preferred_element_type=jnp.float32)


def keep_shares(place, done_ref, weight_ref, keep_ref):
    for turn, share in enumerate(shares(place, place[1], done_ref, weight_ref)):
        keep_ref[turn] = share


def add_pair(keep_ref, other_ref, *out_refs):
    for turn, out_ref in enumerate(out_refs):
        out_ref[...] = (keep_ref[turn] + other_ref[turn].astype(jnp.float32)).astype(jnp.bfloat16)


def run_stage(queries, marks, pieces, state=None, weight=None, place=None):
    first, final = state is None, weight is not None
    arrays, layout = [], []
    for piece in pieces:
        if isinstance(piece, tuple):
            layout.append((len(arrays), 0, len(arrays) + 1, 0))
            arrays.extend(piece)
        else:
            for row in range(0, piece.shape[0], PIECE):
                layout.append((len(arrays), row, len(arrays), row + HALF))
            arrays.append(piece)
    total = len(layout)
    vmem = pl.BlockSpec(memory_space=pltpu.VMEM)
    args = ([place] if final else []) + [queries, marks, *arrays] + ([] if first else list(state))
    in_specs = [vmem] * len(args)
    if final:
        in_specs[0] = pl.BlockSpec(memory_space=pltpu.SMEM)
        args.append(weight)
        in_specs.append(vmem)
        out_shape = [
            jax.ShapeDtypeStruct((ROWS, TOK, COLS), jnp.bfloat16),
            jax.ShapeDtypeStruct((TOK, COLS), jnp.bfloat16),
        ]
    else:
        out_shape = [
            jax.ShapeDtypeStruct((TOK, GROUP), jnp.float32),
            jax.ShapeDtypeStruct((TOK, COLS), jnp.float32),
            jax.ShapeDtypeStruct((TOK, COLS), jnp.float32),
        ]
    flops = EFFORT * 4 * TOK * TOK * COLS * total + (2 * TOK * COLS * COLS * ROWS if final else 0)
    return pl.pallas_call(
        functools.partial(attend_stage, first, final, len(arrays), tuple(layout)),
        out_shape=out_shape,
        in_specs=in_specs,
        out_specs=[vmem] * len(out_shape),
        compiler_params=pltpu.CompilerParams(vmem_limit_bytes=40 << 20),
        cost_estimate=pl.CostEstimate(
            flops=flops,
            bytes_accessed=total * PIECE * TOK * 2 + (8 << 20 if final else 2 << 20),
            transcendentals=total * GROUP * TOK * TOK,
        ),
    )(*args)


def along(value, by):
    size = lax.axis_size("tok")
    return lax.ppermute(value, "tok", [(i, (i + by) % size) for i in range(size)])


def around(value, by):
    size = lax.axis_size("head")
    return lax.ppermute(value, "head", [(i, (i + by) % size) for i in range(size)])


def after(value, earlier):
    return lax.optimization_barrier((value, earlier))


def gather_and_attend(queries, marks, own, weight, place):
    back4 = along(own, 4)
    state = run_stage(queries, marks, [own])
    own, state = after(own, state)
    back1 = along(own, 1)
    back8 = along(back4, 4)
    state = run_stage(queries, marks, [back4], state)
    back4, state = after(back4, state)
    back2, back3, back5 = [along(back4, n) for n in (-2, -1, 1)]
    back12 = along(back8, 4)
    state = run_stage(queries, marks, [back8, back1], state)
    back8, state = after(back8, state)
    back6, back7, back9 = [along(back8, n) for n in (-2, -1, 1)]
    back15, back10, back14 = [along(back12, n) for n in (3, -2, 2)]
    back11, back13 = [along(back12, n) for n in (-1, 1)]
    near = [back5, back3, back2, back9, back7, back6, back12]
    state = run_stage(queries, marks, near, state)
    state = run_stage(queries, marks, [back10, back15], state)
    return run_stage(queries, marks, [back13, back11, back14], state, weight, place)


def join(key_ref, value_ref, ids_ref, joined_ref):
    joined_ref[:TOK, :HEAD_DIM] = key_ref[...]
    joined_ref[:TOK, HEAD_DIM:] = value_ref[...]
    ids = ids_ref[...].astype(jnp.float32)
    joined_ref[TOK:] = jnp.broadcast_to(ids, (MARK, TOK)).astype(jnp.bfloat16)


def per_device(queries, key_heads, value_heads, doc_ids, out_weight):
    own = pl.pallas_call(join, out_shape=jax.ShapeDtypeStruct((PIECE, TOK), jnp.bfloat16))(
        key_heads, value_heads, doc_ids[None]
    )
    own, ids = after(own, doc_ids)
    marks = ids.astype(jnp.float32)
    place = jnp.stack([lax.axis_index("head"), lax.axis_index("srv")]).astype(jnp.int32)
    send, done = gather_and_attend(queries, marks[:, None], own, out_weight, place)
    other = lax.ppermute(send, "srv", [(0, 1), (1, 0)])
    vmem = pl.BlockSpec(memory_space=pltpu.VMEM)
    keep = pl.pallas_call(
        keep_shares,
        out_shape=jax.ShapeDtypeStruct((ROWS, TOK, COLS), jnp.float32),
        in_specs=[pl.BlockSpec(memory_space=pltpu.SMEM), vmem, vmem],
        out_specs=vmem,
        compiler_params=pltpu.CompilerParams(vmem_limit_bytes=40 << 20),
        cost_estimate=pl.CostEstimate(
            flops=2 * 2 * TOK * COLS * COLS * ROWS, bytes_accessed=6 << 20, transcendentals=0
        ),
    )(place, done, out_weight)
    pair = pl.pallas_call(
        add_pair,
        out_shape=[jax.ShapeDtypeStruct((TOK, COLS), jnp.bfloat16)] * ROWS,
        in_specs=[vmem, vmem],
        out_specs=[vmem] * ROWS,
        compiler_params=pltpu.CompilerParams(vmem_limit_bytes=40 << 20),
    )(keep, other)
    summed = pair[0].astype(jnp.float32)
    for turn in (2, 1, 3):
        summed = summed + around(pair[turn], turn).astype(jnp.float32)
    return summed.astype(jnp.bfloat16)


def solution(mesh):
    placed = (
        P("tok", ("head", "srv")),
        P("tok", ("head", "srv")),
        P("tok", ("head", "srv")),
        P("tok"),
        P(("head", "srv"), None),
    )
    return jax.shard_map(
        per_device, mesh=mesh, in_specs=placed, out_specs=P("tok", ("head", "srv")), check_vma=False
    )
```

```python
import functools
import math

import jax
import jax.numpy as jnp
from jax import lax
from jax.experimental import pallas as pl
from jax.experimental.pallas import tpu as pltpu
from jax.sharding import PartitionSpec as P

HEAD_DIM = 128
GROUP = 4
TOK = 256
MARK = 16
HALF = TOK // 2
PIECE = TOK + MARK
COLS = GROUP * HEAD_DIM
ROWS = 4
HIDDEN = -1e30
EFFORT = 6
SCORE_SCALE = math.log2(math.e) / math.sqrt(HEAD_DIM)


def attend_stage(first, final, amount, layout, *refs):
    refs = list(refs)
    place = refs.pop(0) if final else None
    q_ref, mark_ref = refs[:2]
    refs = refs[2:]
    pieces, refs = refs[:amount], refs[amount:]
    if not first:
        top_ref, sum_ref, acc_ref = refs[:3]
        refs = refs[3:]
    if final:
        weight_ref, send_ref, done_ref = refs
    else:
        top_out, sum_out, acc_out = refs

    marks = jnp.broadcast_to(mark_ref[...], (TOK, TOK))
    for h in range(GROUP):
        cols = slice(h * HEAD_DIM, (h + 1) * HEAD_DIM)
        query = q_ref[:, cols]
        scored = []
        for upper, row, lower, start in layout:
            above = pieces[upper][row : row + HALF]
            below = pieces[lower][start : start + HALF]
            both = jnp.concatenate([above, below], axis=0)
            key, value = both[:, :HEAD_DIM], both[:, HEAD_DIM:]
            key_mark = pieces[lower][start + HALF : start + HALF + MARK].astype(jnp.float32)[:1]
            score = lax.dot_general(
                query, key, (((1,), (1,)), ((), ())), preferred_element_type=jnp.float32
            )
            allowed = marks == key_mark
            if first and not scored:
                down = lax.broadcasted_iota(jnp.int32, (TOK, TOK), 0)
                across = lax.broadcasted_iota(jnp.int32, (TOK, TOK), 1)
                allowed = allowed & (across <= down)
            scored.append((jnp.where(allowed, score * SCORE_SCALE, HIDDEN), value))
        highest = None
        for score, _ in scored:
            half = jnp.maximum(score[:, :HEAD_DIM], score[:, HEAD_DIM:])
            highest = half if highest is None else jnp.maximum(highest, half)
        top = jnp.max(highest, axis=1, keepdims=True)
        if not first:
            top = jnp.maximum(top, top_ref[:, h : h + 1])
        total = product = None
        for score, value in scored:
            weight = jnp.exp2(score - top)
            part = weight[:, :HEAD_DIM] + weight[:, HEAD_DIM:]
            total = part if total is None else total + part
            term = jnp.dot(weight.astype(jnp.bfloat16), value, preferred_element_type=jnp.float32)
            product = term if product is None else product + term
        if not first:
            factor = jnp.exp2(top_ref[:, h : h + 1] - top)
            total = total + sum_ref[:, cols] * factor
            product = product + acc_ref[:, cols] * factor
        if final:
            whole = jnp.sum(total, axis=1, keepdims=True)
            done_ref[:, cols] = (product / whole).astype(jnp.bfloat16)
        else:
            top_out[:, h : h + 1] = top
            sum_out[:, cols] = total
            acc_out[:, cols] = product
    if final:
        for turn, share in enumerate(shares(place, 1 - place[1], done_ref, weight_ref)):
            send_ref[turn] = share.astype(jnp.bfloat16)


def shares(place, core, done_ref, weight_ref):
    for turn in range(ROWS):
        block = lax.rem(place[0] + turn, ROWS) * 2 + core
        cols = pl.ds(pl.multiple_of(block * COLS, COLS), COLS)
        yield jnp.dot(done_ref[...], weight_ref[:, cols], preferred_element_type=jnp.float32)


def keep_shares(place, done_ref, weight_ref, keep_ref):
    for turn, share in enumerate(shares(place, place[1], done_ref, weight_ref)):
        keep_ref[turn] = share


def add_pair(keep_ref, other_ref, *out_refs):
    for turn, out_ref in enumerate(out_refs):
        out_ref[...] = (keep_ref[turn] + other_ref[turn].astype(jnp.float32)).astype(jnp.bfloat16)


def run_stage(queries, marks, pieces, state=None, weight=None, place=None):
    first, final = state is None, weight is not None
    arrays, layout = [], []
    for piece in pieces:
        if isinstance(piece, tuple):
            layout.append((len(arrays), 0, len(arrays) + 1, 0))
            arrays.extend(piece)
        else:
            for row in range(0, piece.shape[0], PIECE):
                layout.append((len(arrays), row, len(arrays), row + HALF))
            arrays.append(piece)
    total = len(layout)
    vmem = pl.BlockSpec(memory_space=pltpu.VMEM)
    args = ([place] if final else []) + [queries, marks, *arrays] + ([] if first else list(state))
    in_specs = [vmem] * len(args)
    if final:
        in_specs[0] = pl.BlockSpec(memory_space=pltpu.SMEM)
        args.append(weight)
        in_specs.append(vmem)
        out_shape = [
            jax.ShapeDtypeStruct((ROWS, TOK, COLS), jnp.bfloat16),
            jax.ShapeDtypeStruct((TOK, COLS), jnp.bfloat16),
        ]
    else:
        out_shape = [
            jax.ShapeDtypeStruct((TOK, GROUP), jnp.float32),
            jax.ShapeDtypeStruct((TOK, COLS), jnp.float32),
            jax.ShapeDtypeStruct((TOK, COLS), jnp.float32),
        ]
    flops = EFFORT * 4 * TOK * TOK * COLS * total + (2 * TOK * COLS * COLS * ROWS if final else 0)
    return pl.pallas_call(
        functools.partial(attend_stage, first, final, len(arrays), tuple(layout)),
        out_shape=out_shape,
        in_specs=in_specs,
        out_specs=[vmem] * len(out_shape),
        compiler_params=pltpu.CompilerParams(vmem_limit_bytes=40 << 20),
        cost_estimate=pl.CostEstimate(
            flops=flops,
            bytes_accessed=total * PIECE * TOK * 2 + (8 << 20 if final else 2 << 20),
            transcendentals=total * GROUP * TOK * TOK,
        ),
    )(*args)


def along(value, by):
    size = lax.axis_size("tok")
    return lax.ppermute(value, "tok", [(i, (i + by) % size) for i in range(size)])


def around(value, by):
    size = lax.axis_size("head")
    return lax.ppermute(value, "head", [(i, (i + by) % size) for i in range(size)])


def after(value, earlier):
    return lax.optimization_barrier((value, earlier))


def gather_and_attend(queries, marks, own, weight, place):
    back4 = along(own, 4)
    state = run_stage(queries, marks, [own])
    own, state = after(own, state)
    back1 = along(own, 1)
    back8 = along(back4, 4)
    state = run_stage(queries, marks, [back4], state)
    back4, state = after(back4, state)
    back2, back3, back5 = [along(back4, n) for n in (-2, -1, 1)]
    back12 = along(back8, 4)
    state = run_stage(queries, marks, [back8, back1], state)
    back8, state = after(back8, state)
    back6, back7, back9 = [along(back8, n) for n in (-2, -1, 1)]
    back15, back10, back14 = [along(back12, n) for n in (3, -2, 2)]
    back11, back13 = [along(back12, n) for n in (-1, 1)]
    near = [back5, back3, back2, back9, back7, back6, back12, back10, back15]
    state = run_stage(queries, marks, near, state)
    return run_stage(queries, marks, [back13, back11, back14], state, weight, place)


def join(key_ref, value_ref, ids_ref, joined_ref):
    joined_ref[:TOK, :HEAD_DIM] = key_ref[...]
    joined_ref[:TOK, HEAD_DIM:] = value_ref[...]
    ids = ids_ref[...].astype(jnp.float32)
    joined_ref[TOK:] = jnp.broadcast_to(ids, (MARK, TOK)).astype(jnp.bfloat16)


def per_device(queries, key_heads, value_heads, doc_ids, out_weight):
    own = pl.pallas_call(join, out_shape=jax.ShapeDtypeStruct((PIECE, TOK), jnp.bfloat16))(
        key_heads, value_heads, doc_ids[None]
    )
    own, ids = after(own, doc_ids)
    marks = ids.astype(jnp.float32)
    place = jnp.stack([lax.axis_index("head"), lax.axis_index("srv")]).astype(jnp.int32)
    send, done = gather_and_attend(queries, marks[:, None], own, out_weight, place)
    other = lax.ppermute(send, "srv", [(0, 1), (1, 0)])
    vmem = pl.BlockSpec(memory_space=pltpu.VMEM)
    keep = pl.pallas_call(
        keep_shares,
        out_shape=jax.ShapeDtypeStruct((ROWS, TOK, COLS), jnp.float32),
        in_specs=[pl.BlockSpec(memory_space=pltpu.SMEM), vmem, vmem],
        out_specs=vmem,
        compiler_params=pltpu.CompilerParams(vmem_limit_bytes=40 << 20),
        cost_estimate=pl.CostEstimate(
            flops=2 * 2 * TOK * COLS * COLS * ROWS, bytes_accessed=6 << 20, transcendentals=0
        ),
    )(place, done, out_weight)
    pair = pl.pallas_call(
        add_pair,
        out_shape=[jax.ShapeDtypeStruct((TOK, COLS), jnp.bfloat16)] * ROWS,
        in_specs=[vmem, vmem],
        out_specs=[vmem] * ROWS,
        compiler_params=pltpu.CompilerParams(vmem_limit_bytes=40 << 20),
    )(keep, other)
    summed = pair[0].astype(jnp.float32)
    for turn in (2, 1, 3):
        summed = summed + around(pair[turn], turn).astype(jnp.float32)
    return summed.astype(jnp.bfloat16)


def solution(mesh):
    placed = (
        P("tok", ("head", "srv")),
        P("tok", ("head", "srv")),
        P("tok", ("head", "srv")),
        P("tok"),
        P(("head", "srv"), None),
    )
    return jax.shard_map(
        per_device, mesh=mesh, in_specs=placed, out_specs=P("tok", ("head", "srv")), check_vma=False
    )
```
